256 devices in a mesh: pert: 64 (over z_hi, x, y), gz: 4 (over z_lo, core).
Axes of the slice: x: 4, y: 4, z: 8 (z_hi: 4, z_lo: 2; z = z_hi * 2 + z_lo), core: 2. Of those that a mesh axis runs over, the one named last changes fastest.
Arguments:
- base_store: float32 [64, 4, 64, 1024], P('pert', None, 'gz'), may hold values from -6 to 6
- perturbations: float32 [128, 4, 64, 1024], P('pert', None, 'gz'), may hold values from -6 to 6
- owner_steps: int32 [3], replicated, may hold values from 0 to 63
- w_in: bfloat16 [64, 108], replicated, may hold values from -0.625 to 0.625
- b_in: float32 [64], replicated, may hold values from -4 to 4
- w_mid: bfloat16 [64, 64], replicated, may hold values from -0.75 to 0.75
- b_mid: float32 [64], replicated, may hold values from -4 to 4
- w_out: bfloat16 [6, 64], replicated, may hold values from -2 to 2
Outputs:
- evolved: float32 [128, 4, 64, 1024], P('pert', None, 'gz')
The draws below stay inside these ranges and needn't reach their ends.
Inputs may be any that keep to these rules, and one draw needn't show every extreme that they name: `owner_steps`: index along pert of the device that stores each step's base state.
All inputs are finite; a program needn't handle non-finite values.
Results may differ from the reference program's by a relative error of at most 0.0033.
Values sent between devices are 32-bit elements; how exact they have to be, the bound alone decides.
No kernel may reach another device: no remote copies, remote signals or barrier semaphores. Data moves between devices by JAX's collectives and lax.ppermute only.
A program may use at most 64 MiB of HBM per device.

```python
import jax
import jax.numpy as jnp
from jax import lax

NH = 32
STEPS = 3
FIELDS = 4
INPUTS = 108
UNITS = 64
STRESSES = 6
PERTS = 128
NZ = 64
PLANE = 1024
N_PERT = 64


def steps_of(own_key, shape, shards, low, top_value):
    loudness = 1.0
    for dim, shards_of in shards:
        steps = jax.random.uniform(jax.random.fold_in(jax.random.fold_in(own_key, 6), dim), (shards_of,), jnp.float32, low / len(shards), top_value / len(shards))
        loudness = loudness * jnp.repeat(jnp.exp(steps), shape[dim] // shards_of).reshape((-1,) + (1,) * (len(shape) - 1 - dim))
    return loudness


def scatter_about(key, shape, scale, bound, cuts=(), held_as=jnp.bfloat16):
    loudness = steps_of(key, shape, cuts, -0.22, 0.18) if cuts else 1.0
    result = jax.random.normal(key, shape, jnp.float32) * scale * loudness
    return jnp.minimum(jnp.maximum(result, -bound), bound).astype(held_as)


def setup_inputs(seed: int = 0) -> dict:
    seeds = jax.random.split(jax.random.key(seed), 9)
    base_store = scatter_about(seeds[0], (N_PERT, FIELDS, NZ, PLANE), 1.0, 6.0, ((0, 64), (2, 4)), jnp.float32)
    perturbations = scatter_about(seeds[1], (PERTS, FIELDS, NZ, PLANE), 1.0, 6.0, ((0, 64), (2, 4)), jnp.float32)
    owner_steps = jax.random.randint(seeds[2], (STEPS,), 0, N_PERT).astype(jnp.int32)
    w_in = scatter_about(seeds[3], (UNITS, INPUTS), INPUTS ** -0.5, 0.625)
    b_in = scatter_about(seeds[4], (UNITS,), 1.0, 4.0, (), jnp.float32)
    w_mid = scatter_about(seeds[5], (UNITS, UNITS), UNITS ** -0.5, 0.75)
    b_mid = scatter_about(seeds[6], (UNITS,), 1.0, 4.0, (), jnp.float32)
    w_out = scatter_about(seeds[7], (STRESSES, UNITS), 8 ** -0.5, 2.0)
    return dict(base_store=base_store, perturbations=perturbations, owner_steps=owner_steps, w_in=w_in, b_in=b_in, w_mid=w_mid, b_mid=b_mid, w_out=w_out)


TIME_STEP = 0.2


def along_x(field, offset):
    if offset == 0:
        return field
    return jnp.roll(field, -offset * NH, axis=-1)


def along_y(field, offset):
    if offset == 0:
        return field
    plain = jnp.roll(field, -offset, axis=-1)
    wrapped = jnp.roll(field, offset * NH - offset, axis=-1)
    column = jnp.arange(field.shape[-1], dtype=jnp.int32) % NH
    edge = column == (NH - 1 if offset > 0 else 0)
    return jnp.where(edge, wrapped, plain)


def patch_of(slab):
    pieces = []
    for zed in range(3):
        layer_slab = slab[..., zed, :]
        for xed in range(3):
            for yed in range(3):
                pieces.append(along_x(along_y(layer_slab, yed - 1), xed - 1))
    stacked = jnp.stack(pieces, axis=-3)
    return stacked.reshape(stacked.shape[:-3] + (108, stacked.shape[-1]))


def stress_plane(base_pad, pert_pad, center, w_in, b_in, w_mid, b_mid, w_out):
    base_slab = lax.dynamic_slice_in_dim(base_pad, center - 1, 3, axis=1).astype(jnp.bfloat16)
    base_patch = patch_of(base_slab)
    pert_slab = lax.dynamic_slice_in_dim(pert_pad, center - 1, 3, axis=2).astype(jnp.bfloat16)
    pert_patch = patch_of(pert_slab)
    first = jnp.tanh(jnp.dot(w_in, base_patch, preferred_element_type=jnp.float32) + b_in[:, None])
    second = jnp.tanh(jnp.dot(w_mid, first.astype(jnp.bfloat16), preferred_element_type=jnp.float32) + b_mid[:, None])
    slope_first = 1.0 - first * first
    slope_second = 1.0 - second * second
    lin_one = jnp.einsum("hk,pkc->phc", w_in.astype(jnp.float32), pert_patch.astype(jnp.float32))
    lift_one = (slope_first * lin_one).astype(jnp.bfloat16)
    lin_two = jnp.einsum("hk,pkc->phc", w_mid.astype(jnp.float32), lift_one.astype(jnp.float32))
    lift_two = (slope_second * lin_two).astype(jnp.bfloat16)
    return jnp.einsum("hk,pkc->phc", w_out.astype(jnp.float32), lift_two.astype(jnp.float32))


def advect(base_one, pert_one):
    total = None
    for direction in range(3):
        flux = base_one[direction] * pert_one + pert_one[:, direction:direction + 1] * base_one
        if direction == 0:
            inner = flux[:, :, 1:-1]
            change = along_x(inner, 1) - along_x(inner, -1)
        elif direction == 1:
            inner = flux[:, :, 1:-1]
            change = along_y(inner, 1) - along_y(inner, -1)
        else:
            change = flux[:, :, 2:] - flux[:, :, :-2]
        total = change if total is None else total + change
    return -total


def closure(stress_pad):
    inner = stress_pad[:, :, 1:-1]

    def diff_x(comp):
        return along_x(inner[:, comp], 1) - along_x(inner[:, comp], -1)

    def diff_y(comp):
        return along_y(inner[:, comp], 1) - along_y(inner[:, comp], -1)

    def diff_z(comp):
        return stress_pad[:, comp, 2:] - stress_pad[:, comp, :-2]

    first_row = diff_x(0) + diff_y(3) + diff_z(4)
    second_row = diff_x(3) + diff_y(1) + diff_z(5)
    third_row = diff_x(4) + diff_y(5) + diff_z(2)
    return jnp.stack([first_row, second_row, third_row, jnp.zeros_like(first_row)], axis=1)


def reference(base_store, perturbations, owner_steps, w_in, b_in, w_mid, b_mid, w_out):
    state = perturbations
    plane_count = state.shape[2]
    for step_index in range(STEPS):
        base = base_store[owner_steps[step_index]]
        base_pad = jnp.pad(base, ((0, 0), (1, 1), (0, 0)))
        pert_pad = jnp.pad(state, ((0, 0), (0, 0), (1, 1), (0, 0)))

        def one_plane(center):
            return stress_plane(base_pad, pert_pad, center, w_in, b_in, w_mid, b_mid, w_out)

        centers = jnp.arange(1, plane_count + 1, dtype=jnp.int32)
        stress = jnp.transpose(lax.map(one_plane, centers), (1, 2, 0, 3))
        stress_pad = jnp.pad(stress, ((0, 0), (0, 0), (1, 1), (0, 0)))
        state = state + TIME_STEP * (advect(base_pad, pert_pad) + closure(stress_pad))
    return state
```

```python
import functools

import jax
import jax.numpy as jnp
from jax import lax
from jax.experimental import pallas as pl
from jax.experimental.pallas import tpu as pltpu
from jax.sharding import Mesh, PartitionSpec as P

NH = 32
STEPS = 3
TIME_STEP = 0.2
PLANES = 16
HALO = 6
EXT = PLANES + 2 * HALO
BLOCK = 8
SHIFT = BLOCK - HALO
PLANE = 1024
UNITS = 64
LANES = 128
CHUNK = 256
PROWS = 80
BROWS = 48


def shift_y(v, column):
    up = jnp.where(column == NH - 1, pltpu.roll(v, NH - 1, 1), pltpu.roll(v, LANES - 1, 1))
    down = jnp.where(column == 0, pltpu.roll(v, LANES - NH + 1, 1), pltpu.roll(v, 1, 1))
    return down, up


def shift_x(parts, lane):
    n = len(parts)
    left = [pltpu.roll(v, LANES - NH, 1) for v in parts]
    right = [pltpu.roll(v, NH, 1) for v in parts]
    up = [jnp.where(lane < LANES - NH, left[k], left[(k + 1) % n]) for k in range(n)]
    down = [jnp.where(lane >= NH, right[k], right[(k - 1) % n]) for k in range(n)]
    return down, up


def kernel(place, own, low, high, r0, r1, r2, r3, wp, wb, wm, wm2, wo, b_in, b_mid, out,
           st, base, pp, bp, part, gz, bias):
    f32, bf16 = jnp.float32, jnp.bfloat16
    lane = lax.broadcasted_iota(jnp.int32, (8, LANES), 1)
    column = lane % NH
    upper = lax.broadcasted_iota(jnp.int32, (8, LANES), 0) < 4
    upper_wide = lax.broadcasted_iota(jnp.int32, (8, CHUNK), 0) < 4
    parts = PLANE // LANES
    y_now, slab, slabs = place[0], place[1], place[2]

    st[0:HALO] = low[...]
    st[HALO : HALO + PLANES] = own[...]
    st[HALO + PLANES :] = high[...]
    bias[0] = jnp.broadcast_to(b_in[...], (UNITS, CHUNK))
    bias[1] = jnp.broadcast_to(b_mid[...], (UNITS, CHUNK))
    pad = jnp.zeros((8, LANES), f32)

    def inside(e):
        level = slab * PLANES + e - HALO
        return jnp.logical_and(level >= 0, level < slabs * PLANES)

    for step in range(STEPS):
        lo, hi = 2 * step, EXT - 2 * step

        for k, ref in enumerate((r0, r1, r2, r3)):
            start = lax.rem(y_now + 4 - k, 4) * BLOCK

            @pl.loop(0, BLOCK)
            def _(z):
                rows = ref[step, z]
                base[start + z, 0:4] = rows
                base[start + z, 4:8] = rows

        @pl.loop(lo, hi)
        def _(e):
            mid = [st[e, :, k * LANES : (k + 1) * LANES] for k in range(parts)]
            moved = [shift_y(v, column) for v in mid]
            rows = []
            thirds = [[m[0] for m in moved], mid, [m[1] for m in moved]]
            moved_x = [shift_x(third, lane) for third in thirds]
            for xed in range(3):
                for yed in range(3):
                    rows.append(thirds[yed] if xed == 1 else moved_x[yed][xed // 2])
            for t in range(5):
                for k in range(parts):
                    second = rows[2 * t + 1][k] if 2 * t + 1 < 9 else pad
                    pair = jnp.concatenate([rows[2 * t][k], second], axis=0)
                    pp[e, 16 * t : 16 * t + 16, k * LANES : (k + 1) * LANES] = pair.astype(bf16)
            mid = [base[e + SHIFT, :, k * LANES : (k + 1) * LANES] for k in range(parts)]
            both = []
            for v in mid:
                down, up = shift_y(v, column)
                both.append(jnp.where(upper, down, up))
            both_down, both_up = shift_x(both, lane)
            mid_down, mid_up = shift_x(mid, lane)
            sides = [jnp.where(upper, a, b) for a, b in zip(mid_down, mid_up)]
            rows = [both_down, both, both_up, sides, mid, [pad] * parts]
            for t in range(3):
                for k in range(parts):
                    pair = jnp.concatenate([rows[2 * t][k], rows[2 * t + 1][k]], axis=0)
                    bp[e, 16 * t : 16 * t + 16, k * LANES : (k + 1) * LANES] = pair.astype(bf16)

        @pl.loop(lo + 1, hi - 1)
        def _(e):
            keep = inside(e)
            gx, gy = [], []
            for n in range(PLANE // CHUNK):
                cells = slice(n * CHUNK, (n + 1) * CHUNK)
                patch = pp[pl.ds(e - 1, 3), :, cells].reshape(3 * PROWS, CHUNK)
                base_patch = bp[pl.ds(e - 1, 3), :, cells].reshape(3 * BROWS, CHUNK)
                first = jnp.tanh(jnp.dot(wb[...], base_patch, preferred_element_type=f32) + bias[0])
                second = jnp.tanh(
                    jnp.dot(wm[...], first.astype(bf16), preferred_element_type=f32) + bias[1]
                )
                slope_first = 1.0 - first * first
                slope_second = 1.0 - second * second
                lin_one = jnp.dot(wp[...], patch, preferred_element_type=f32)
                lift_one = jnp.concatenate(
                    [slope_first * lin_one[:UNITS], slope_first * lin_one[UNITS:]], axis=0
                ).astype(bf16)
                lin_two = jnp.dot(wm2[...], lift_one, preferred_element_type=f32)
                lift_two = jnp.concatenate(
                    [slope_second * lin_two[:UNITS], slope_second * lin_two[UNITS:]], axis=0
                ).astype(bf16)
                stress = jnp.dot(wo[...], lift_two, preferred_element_type=f32)
                stress = jnp.where(keep, stress, 0.0)
                v = st[e, :, cells]
                u = base[e + SHIFT, :, cells]
                g = []
                for j in range(3):
                    u_j = base[e + SHIFT, j : j + 1, cells]
                    v_j = jnp.where(upper_wide, st[e, j : j + 1, cells], st[e, 4 + j : 5 + j, cells])
                    g.append(stress[8 * j : 8 * j + 8] - (u_j * v + v_j * u))
                gz[e, :, cells] = g[2]
                for half in range(CHUNK // LANES):
                    gx.append(g[0][:, half * LANES : (half + 1) * LANES])
                    gy.append(g[1][:, half * LANES : (half + 1) * LANES])
            down_x, up_x = shift_x(gx, lane)
            for k in range(parts):
                down_y, up_y = shift_y(gy[k], column)
                part[e, :, k * LANES : (k + 1) * LANES] = (up_x[k] - down_x[k]) + (up_y - down_y)

        @pl.loop(lo + 2, hi - 2)
        def _(e):
            new = st[e] + TIME_STEP * (part[e] + (gz[e + 1] - gz[e - 1]))
            if step == STEPS - 1:
                out[e - HALO] = new
            else:
                st[e] = jnp.where(inside(e), new, 0.0)


def weights_of(w_in, w_mid, w_out):
    bf16 = jnp.bfloat16
    eye = jnp.eye(2, dtype=bf16)
    split = jnp.pad(w_in.reshape(UNITS, 3, 9, 4), ((0, 0), (0, 0), (0, 1), (0, 0)))
    wp = eye[:, None, None, None, :, None] * split[None, :, :, :, None, :]
    wp = wp.reshape(2 * UNITS, 3 * PROWS)
    order = (0, 2, 3, 5, 6, 8, 1, 7, 4, 9, 9, 9)
    wb = jnp.concatenate([split[:, :, i : i + 1] for i in order], axis=2).reshape(UNITS, 3 * BROWS)
    wm2 = (eye[:, None, :, None] * w_mid[None, :, None, :]).reshape(2 * UNITS, 2 * UNITS)
    out_pad = jnp.pad(w_out, ((0, 1), (0, 0)))
    comps = (0, 3, 4, 6, 3, 1, 5, 6, 4, 5, 2, 6)
    rows = jnp.concatenate([out_pad[i : i + 1] for i in comps], axis=0).reshape(3, 1, 4, 1, UNITS)
    wo = (rows * eye[None, :, None, :, None]).reshape(24, 2 * UNITS)
    return wp, wb, w_mid, wm2, wo


def pick(options, which):
    chosen = options[0]
    for k in range(1, len(options)):
        chosen = jnp.where(which == k, options[k], chosen)
    return chosen


def around(piece, axis):
    return [piece] + [
        lax.ppermute(piece, axis, [(i, (i + k) % 4) for i in range(4)]) for k in (1, 2, 3)
    ]


def spread_base(base_store, owner_steps, slabs):
    x, y, h = (lax.axis_index(a) for a in ("x", "y", "h"))
    owner_h, owner_x, owner_y = (owner_steps // 16, (owner_steps // 4) % 4, owner_steps % 4)
    blocks = jnp.transpose(base_store[0].reshape(4, 2, BLOCK, PLANE), (1, 2, 0, 3))
    come = []
    for k in range(4):
        pairs = []
        for target in range(4):
            source = (target - k) % 4
            for slab in range(slabs):
                other = slab + (-1, 0, 0, 1)[target]
                if 0 <= other < slabs:
                    pairs.append((source * slabs + other, target * slabs + slab))
        target = (y + k) % 4
        send = jnp.where(target % 2 == 0, blocks[1], blocks[0])
        come.append(lax.ppermute(send, ("y", "gz"), pairs))
    mine = jnp.stack([pick(come, (y - owner_y[s]) % 4) for s in range(STEPS)])
    width = PLANE // 4

    def cells_of(which):
        return lax.dynamic_slice_in_dim(mine, which * width, width, axis=3)

    come = [cells_of(x)]
    for k in (1, 2, 3):
        pairs = [(i, (i + k) % 4) for i in range(4)]
        come.append(lax.ppermute(cells_of((x + k) % 4), "x", pairs))
    mine = jnp.stack([pick([c[s] for c in come], (x - owner_x[s]) % 4) for s in range(STEPS)])
    come = around(mine, "h")
    mine = jnp.stack([pick([c[s] for c in come], (h - owner_h[s]) % 4) for s in range(STEPS)])
    come = around(mine, "x")
    ring = [come[0], come[3], come[2], come[1]]
    whole = jnp.concatenate([pick([ring[(j - i) % 4] for i in range(4)], x) for j in range(4)], axis=3)
    return around(whole, "y")


def local(base_store, perturbations, owner_steps, w_in, b_in, w_mid, b_mid, w_out):
    slabs = lax.axis_size("gz")
    slab = lax.axis_index("gz")
    state = jnp.transpose(perturbations.reshape(8, PLANES, PLANE), (1, 0, 2))
    up = [(i, i + 1) for i in range(slabs - 1)]
    down = [(j, i) for i, j in up]
    low = lax.ppermute(state[PLANES - HALO :], "gz", up)
    high = lax.ppermute(state[:HALO], "gz", down)
    come = spread_base(base_store, owner_steps, slabs)
    place = jnp.stack([lax.axis_index("y"), slab, jnp.int32(slabs)]).astype(jnp.int32)
    vmem = pl.BlockSpec(memory_space=pltpu.VMEM)
    f32, bf16 = jnp.float32, jnp.bfloat16
    new = pl.pallas_call(
        kernel,
        out_shape=jax.ShapeDtypeStruct((PLANES, 8, PLANE), f32),
        in_specs=[pl.BlockSpec(memory_space=pltpu.SMEM)] + [vmem] * 14,
        out_specs=vmem,
        scratch_shapes=[
            pltpu.VMEM((EXT, 8, PLANE), f32),
            pltpu.VMEM((4 * BLOCK, 8, PLANE), f32),
            pltpu.VMEM((EXT, PROWS, PLANE), bf16),
            pltpu.VMEM((EXT, BROWS, PLANE), bf16),
            pltpu.VMEM((EXT, 8, PLANE), f32),
            pltpu.VMEM((EXT, 8, PLANE), f32),
            pltpu.VMEM((2, UNITS, CHUNK), f32),
        ],
        compiler_params=pltpu.CompilerParams(vmem_limit_bytes=40 * 2**20),
    )(place, state, low, high, *come, *weights_of(w_in, w_mid, w_out), b_in[:, None], b_mid[:, None])
    return jnp.transpose(new, (1, 0, 2)).reshape(perturbations.shape)


def solution(mesh):
    spec = P(("h", "x", "y"), None, "gz", None)
    fine = Mesh(mesh.devices.reshape(4, 4, 4, mesh.devices.shape[1]), ("h", "x", "y", "gz"))
    in_specs = (spec, spec, P(), P(), P(), P(), P(), P())
    return jax.shard_map(local, mesh=fine, in_specs=in_specs, out_specs=spec, check_vma=False)
```

```python
import functools

import jax
import jax.numpy as jnp
from jax import lax
from jax.experimental import pallas as pl
from jax.experimental.pallas import tpu as pltpu
from jax.sharding import Mesh, PartitionSpec as P

NH = 32
STEPS = 3
TIME_STEP = 0.2
PLANES = 16
HALO = 6
EXT = PLANES + 2 * HALO
BLOCK = 8
SHIFT = BLOCK - HALO
PLANE = 1024
UNITS = 64
LANES = 128
CHUNK = 256
PROWS = 80
BROWS = 48


def shift_y(v, column):
    up = jnp.where(column == NH - 1, pltpu.roll(v, NH - 1, 1), pltpu.roll(v, LANES - 1, 1))
    down = jnp.where(column == 0, pltpu.roll(v, LANES - NH + 1, 1), pltpu.roll(v, 1, 1))
    return down, up


def shift_x(parts, lane):
    n = len(parts)
    left = [pltpu.roll(v, LANES - NH, 1) for v in parts]
    right = [pltpu.roll(v, NH, 1) for v in parts]
    up = [jnp.where(lane < LANES - NH, left[k], left[(k + 1) % n]) for k in range(n)]
    down = [jnp.where(lane >= NH, right[k], right[(k - 1) % n]) for k in range(n)]
    return down, up


def kernel(place, own, low, high, r0, r1, r2, r3, wp, wb, wm, wo, b_in, b_mid, out,
           st, base, pp, bp, part, gz, bias, mid_in, out_in):
    f32, bf16 = jnp.float32, jnp.bfloat16
    lane = lax.broadcasted_iota(jnp.int32, (8, LANES), 1)
    column = lane % NH
    upper = lax.broadcasted_iota(jnp.int32, (8, LANES), 0) < 4
    upper_wide = lax.broadcasted_iota(jnp.int32, (8, CHUNK), 0) < 4
    parts = PLANE // LANES
    y_now, slab, slabs = place[0], place[1], place[2]

    st[0:HALO] = low[...]
    st[HALO : HALO + PLANES] = own[...]
    st[HALO + PLANES : EXT] = high[...]
    bias[0] = jnp.broadcast_to(b_in[...], (UNITS, CHUNK))
    bias[1] = jnp.broadcast_to(b_mid[...], (UNITS, CHUNK))
    pad = jnp.zeros((8, LANES), f32)

    def inside(e):
        level = slab * PLANES + e - HALO
        return jnp.logical_and(level >= 0, level < slabs * PLANES)

    def patches(e):
        mid = [st[e, :, k * LANES : (k + 1) * LANES] for k in range(parts)]
        moved = [shift_y(v, column) for v in mid]
        rows = []
        thirds = [[m[0] for m in moved], mid, [m[1] for m in moved]]
        moved_x = [shift_x(third, lane) for third in thirds]
        for xed in range(3):
            for yed in range(3):
                rows.append(thirds[yed] if xed == 1 else moved_x[yed][xed // 2])
        for t in range(5):
            for k in range(parts):
                second = rows[2 * t + 1][k] if 2 * t + 1 < 9 else pad
                pair = jnp.concatenate([rows[2 * t][k], second], axis=0)
                pp[e, 16 * t : 16 * t + 16, k * LANES : (k + 1) * LANES] = pair.astype(bf16)
        mid = [base[e + SHIFT, :, k * LANES : (k + 1) * LANES] for k in range(parts)]
        both = []
        for v in mid:
            down, up = shift_y(v, column)
            both.append(jnp.where(upper, down, up))
        both_down, both_up = shift_x(both, lane)
        mid_down, mid_up = shift_x(mid, lane)
        sides = [jnp.where(upper, a, b) for a, b in zip(mid_down, mid_up)]
        rows = [both_down, both, both_up, sides, mid, [pad] * parts]
        for t in range(3):
            for k in range(parts):
                pair = jnp.concatenate([rows[2 * t][k], rows[2 * t + 1][k]], axis=0)
                bp[e, 16 * t : 16 * t + 16, k * LANES : (k + 1) * LANES] = pair.astype(bf16)

    def layer_one(e, cells):
        patch = pp[pl.ds(e - 1, 3), :, cells].reshape(3 * PROWS, CHUNK)
        base_patch = bp[pl.ds(e - 1, 3), :, cells].reshape(3 * BROWS, CHUNK)
        first = jnp.tanh(jnp.dot(wb[...], base_patch, preferred_element_type=f32) + bias[0])
        slope = 1.0 - first * first
        lin = jnp.dot(wp[...], patch, preferred_element_type=f32)
        mid_in[0:UNITS, cells] = first.astype(bf16)
        mid_in[UNITS : 2 * UNITS, cells] = (slope * lin[:UNITS]).astype(bf16)
        mid_in[2 * UNITS :, cells] = (slope * lin[UNITS:]).astype(bf16)

    def layer_two(cells):
        lin = jnp.dot(wm[...], mid_in[:, cells], preferred_element_type=f32)
        second = jnp.tanh(lin[:UNITS] + bias[1])
        slope = 1.0 - second * second
        out_in[0:UNITS, cells] = (slope * lin[UNITS : 2 * UNITS]).astype(bf16)
        out_in[UNITS:, cells] = (slope * lin[2 * UNITS :]).astype(bf16)

    def layer_three(e, cells, keep):
        stress = jnp.dot(wo[...], out_in[:, cells], preferred_element_type=f32)
        stress = jnp.where(keep, stress, 0.0)
        v = st[e, :, cells]
        u = base[e + SHIFT, :, cells]
        g = []
        for j in range(3):
            u_j = base[e + SHIFT, j : j + 1, cells]
            v_j = jnp.where(upper_wide, st[e, j : j + 1, cells], st[e, 4 + j : 5 + j, cells])
            g.append(stress[8 * j : 8 * j + 8] - (u_j * v + v_j * u))
        return g

    for step in range(STEPS):
        lo, hi = 2 * step, EXT - 2 * step

        for k, ref in enumerate((r0, r1, r2, r3)):
            start = lax.rem(y_now + 4 - k, 4) * BLOCK

            @pl.loop(0, BLOCK)
            def _(z):
                rows = ref[step, z]
                base[start + z, 0:4] = rows
                base[start + z, 4:8] = rows

        def divergence(e, gx, gy):
            down_x, up_x = shift_x(gx, lane)
            for k in range(parts):
                down_y, up_y = shift_y(gy[k], column)
                part[e, :, k * LANES : (k + 1) * LANES] = (up_x[k] - down_x[k]) + (up_y - down_y)

        def update(e):
            new = st[e] + TIME_STEP * (part[e] + (gz[e + 1] - gz[e - 1]))
            if step == STEPS - 1:
                out[jnp.clip(e - HALO, 0, PLANES - 1)] = new
            else:
                st[e] = jnp.where(inside(e), new, 0.0)

        def body(i, ahead, one, two, three, after):
            gx, gy = [], []
            for n in range(PLANE // CHUNK):
                cells = slice(n * CHUNK, (n + 1) * CHUNK)
                if three:
                    g = layer_three(i - 4, cells, inside(i - 4))
                    gz[i - 4, :, cells] = g[2]
                    for half in range(CHUNK // LANES):
                        gx.append(g[0][:, half * LANES : (half + 1) * LANES])
                        gy.append(g[1][:, half * LANES : (half + 1) * LANES])
                if two:
                    layer_two(cells)
                if one:
                    layer_one(i - 2, cells)
            if three:
                divergence(i - 4, gx, gy)
            if ahead:
                patches(i)
            if after:
                update(i - 6)

        @pl.loop(lo, lo + 3)
        def _(i):
            body(i, True, False, False, False, False)

        body(lo + 3, True, True, False, False, False)
        body(lo + 4, True, True, True, False, False)

        @pl.loop(lo + 5, lo + 8)
        def _(i):
            body(i, True, True, True, True, False)

        @pl.loop(lo + 8, hi)
        def _(i):
            body(i, True, True, True, True, True)

        body(hi, False, True, True, True, True)
        body(hi + 1, False, False, True, True, True)
        body(hi + 2, False, False, False, True, True)
        body(hi + 3, False, False, False, False, True)


def weights_of(w_in, w_mid, w_out):
    bf16 = jnp.bfloat16
    eye = jnp.eye(2, dtype=bf16)
    split = jnp.pad(w_in.reshape(UNITS, 3, 9, 4), ((0, 0), (0, 0), (0, 1), (0, 0)))
    wp = eye[:, None, None, None, :, None] * split[None, :, :, :, None, :]
    wp = wp.reshape(2 * UNITS, 3 * PROWS)
    order = (0, 2, 3, 5, 6, 8, 1, 7, 4, 9, 9, 9)
    wb = jnp.concatenate([split[:, :, i : i + 1] for i in order], axis=2).reshape(UNITS, 3 * BROWS)
    wm = jnp.eye(3, dtype=bf16)[:, None, :, None] * w_mid[None, :, None, :]
    wm = wm.reshape(3 * UNITS, 3 * UNITS)
    out_pad = jnp.pad(w_out, ((0, 1), (0, 0)))
    comps = (0, 3, 4, 6, 3, 1, 5, 6, 4, 5, 2, 6)
    rows = jnp.concatenate([out_pad[i : i + 1] for i in comps], axis=0).reshape(3, 1, 4, 1, UNITS)
    wo = (rows * eye[None, :, None, :, None]).reshape(24, 2 * UNITS)
    return wp, wb, wm, wo


def pick(options, which):
    chosen = options[0]
    for k in range(1, len(options)):
        chosen = jnp.where(which == k, options[k], chosen)
    return chosen


def around(piece, axis):
    return [piece] + [
        lax.ppermute(piece, axis, [(i, (i + k) % 4) for i in range(4)]) for k in (1, 2, 3)
    ]


def spread_base(base_store, owner_steps, slabs):
    x, y, h = (lax.axis_index(a) for a in ("x", "y", "h"))
    owner_h, owner_x, owner_y = (owner_steps // 16, (owner_steps // 4) % 4, owner_steps % 4)
    blocks = jnp.transpose(base_store[0].reshape(4, 2, BLOCK, PLANE), (1, 2, 0, 3))
    come = []
    for k in range(4):
        pairs = []
        for target in range(4):
            source = (target - k) % 4
            for slab in range(slabs):
                other = slab + (-1, 0, 0, 1)[target]
                if 0 <= other < slabs:
                    pairs.append((source * slabs + other, target * slabs + slab))
        target = (y + k) % 4
        send = jnp.where(target % 2 == 0, blocks[1], blocks[0])
        come.append(lax.ppermute(send, ("y", "gz"), pairs))
    mine = jnp.stack([pick(come, (y - owner_y[s]) % 4) for s in range(STEPS)])
    width = PLANE // 4

    def cells_of(which):
        return lax.dynamic_slice_in_dim(mine, which * width, width, axis=3)

    come = [cells_of(x)]
    for k in (1, 2, 3):
        pairs = [(i, (i + k) % 4) for i in range(4)]
        come.append(lax.ppermute(cells_of((x + k) % 4), "x", pairs))
    mine = jnp.stack([pick([c[s] for c in come], (x - owner_x[s]) % 4) for s in range(STEPS)])
    come = around(mine, "h")
    mine = jnp.stack([pick([c[s] for c in come], (h - owner_h[s]) % 4) for s in range(STEPS)])
    come = around(mine, "x")
    ring = [come[0], come[3], come[2], come[1]]
    whole = jnp.concatenate([pick([ring[(j - i) % 4] for i in range(4)], x) for j in range(4)], axis=3)
    return around(whole, "y")


def local(base_store, perturbations, owner_steps, w_in, b_in, w_mid, b_mid, w_out):
    slabs = lax.axis_size("gz")
    slab = lax.axis_index("gz")
    state = jnp.transpose(perturbations.reshape(8, PLANES, PLANE), (1, 0, 2))
    up = [(i, i + 1) for i in range(slabs - 1)]
    down = [(j, i) for i, j in up]
    low = lax.ppermute(state[PLANES - HALO :], "gz", up)
    high = lax.ppermute(state[:HALO], "gz", down)
    come = spread_base(base_store, owner_steps, slabs)
    place = jnp.stack([lax.axis_index("y"), slab, jnp.int32(slabs)]).astype(jnp.int32)
    vmem = pl.BlockSpec(memory_space=pltpu.VMEM)
    f32, bf16 = jnp.float32, jnp.bfloat16
    new = pl.pallas_call(
        kernel,
        out_shape=jax.ShapeDtypeStruct((PLANES, 8, PLANE), f32),
        in_specs=[pl.BlockSpec(memory_space=pltpu.SMEM)] + [vmem] * 13,
        out_specs=vmem,
        scratch_shapes=[
            pltpu.VMEM((EXT, 8, PLANE), f32),
            pltpu.VMEM((4 * BLOCK, 8, PLANE), f32),
            pltpu.VMEM((EXT, PROWS, PLANE), bf16),
            pltpu.VMEM((EXT, BROWS, PLANE), bf16),
            pltpu.VMEM((EXT, 8, PLANE), f32),
            pltpu.VMEM((EXT, 8, PLANE), f32),
            pltpu.VMEM((2, UNITS, CHUNK), f32),
            pltpu.VMEM((3 * UNITS, PLANE), bf16),
            pltpu.VMEM((2 * UNITS, PLANE), bf16),
        ],
        compiler_params=pltpu.CompilerParams(vmem_limit_bytes=40 * 2**20),
    )(place, state, low, high, *come, *weights_of(w_in, w_mid, w_out), b_in[:, None], b_mid[:, None])
    return jnp.transpose(new, (1, 0, 2)).reshape(perturbations.shape)


def solution(mesh):
    spec = P(("h", "x", "y"), None, "gz", None)
    fine = Mesh(mesh.devices.reshape(4, 4, 4, mesh.devices.shape[1]), ("h", "x", "y", "gz"))
    in_specs = (spec, spec, P(), P(), P(), P(), P(), P())
    return jax.shard_map(local, mesh=fine, in_specs=in_specs, out_specs=spec, check_vma=False)
```

```python
import jax
import jax.numpy as jnp
from jax import lax
from jax.experimental import pallas as pl
from jax.experimental.pallas import tpu as pltpu
from jax.sharding import Mesh, PartitionSpec as P

NH = 32
STEPS = 3
TIME_STEP = 0.2
PLANES = 16
HALO = 6
EXT = PLANES + 2 * HALO
PLANE = 1024
UNITS = 64
LANES = 128
CHUNK = 256
PROWS = 80
BROWS = 48


def shift_y(v, column):
    up = jnp.where(column == NH - 1, pltpu.roll(v, NH - 1, 1), pltpu.roll(v, LANES - 1, 1))
    down = jnp.where(column == 0, pltpu.roll(v, LANES - NH + 1, 1), pltpu.roll(v, 1, 1))
    return down, up


def shift_x(parts, lane):
    n = len(parts)
    left = [pltpu.roll(v, LANES - NH, 1) for v in parts]
    right = [pltpu.roll(v, NH, 1) for v in parts]
    up = [jnp.where(lane < LANES - NH, left[k], left[(k + 1) % n]) for k in range(n)]
    down = [jnp.where(lane >= NH, right[k], right[(k - 1) % n]) for k in range(n)]
    return down, up


def kernel(place, own, low, high, base_low, base_own, base_high, wp, wb, wm, wo, b_in, b_mid, out,
           st, base, pp, bp, part, gz, bias, mid_in, out_in):
    f32, bf16 = jnp.float32, jnp.bfloat16
    lane = lax.broadcasted_iota(jnp.int32, (8, LANES), 1)
    column = lane % NH
    upper = lax.broadcasted_iota(jnp.int32, (8, LANES), 0) < 4
    upper_wide = lax.broadcasted_iota(jnp.int32, (8, CHUNK), 0) < 4
    parts = PLANE // LANES
    slab, slabs = place[0], place[1]

    st[0:HALO] = low[...]
    st[HALO : HALO + PLANES] = own[...]
    st[HALO + PLANES : EXT] = high[...]
    bias[0] = jnp.broadcast_to(b_in[...], (UNITS, CHUNK))
    bias[1] = jnp.broadcast_to(b_mid[...], (UNITS, CHUNK))
    pad = jnp.zeros((8, LANES), f32)

    def inside(e):
        level = slab * PLANES + e - HALO
        return jnp.logical_and(level >= 0, level < slabs * PLANES)

    def patches(e):
        mid = [st[e, :, k * LANES : (k + 1) * LANES] for k in range(parts)]
        moved = [shift_y(v, column) for v in mid]
        rows = []
        thirds = [[m[0] for m in moved], mid, [m[1] for m in moved]]
        moved_x = [shift_x(third, lane) for third in thirds]
        for xed in range(3):
            for yed in range(3):
                rows.append(thirds[yed] if xed == 1 else moved_x[yed][xed // 2])
        for t in range(5):
            for k in range(parts):
                second = rows[2 * t + 1][k] if 2 * t + 1 < 9 else pad
                pair = jnp.concatenate([rows[2 * t][k], second], axis=0)
                pp[e, 16 * t : 16 * t + 16, k * LANES : (k + 1) * LANES] = pair.astype(bf16)
        mid = [base[e, :, k * LANES : (k + 1) * LANES] for k in range(parts)]
        both = []
        for v in mid:
            down, up = shift_y(v, column)
            both.append(jnp.where(upper, down, up))
        both_down, both_up = shift_x(both, lane)
        mid_down, mid_up = shift_x(mid, lane)
        sides = [jnp.where(upper, a, b) for a, b in zip(mid_down, mid_up)]
        rows = [both_down, both, both_up, sides, mid, [pad] * parts]
        for t in range(3):
            for k in range(parts):
                pair = jnp.concatenate([rows[2 * t][k], rows[2 * t + 1][k]], axis=0)
                bp[e, 16 * t : 16 * t + 16, k * LANES : (k + 1) * LANES] = pair.astype(bf16)

    def layer_one(e, cells):
        patch = pp[pl.ds(e - 1, 3), :, cells].reshape(3 * PROWS, CHUNK)
        base_patch = bp[pl.ds(e - 1, 3), :, cells].reshape(3 * BROWS, CHUNK)
        first = jnp.tanh(jnp.dot(wb[...], base_patch, preferred_element_type=f32) + bias[0])
        slope = 1.0 - first * first
        lin = jnp.dot(wp[...], patch, preferred_element_type=f32)
        mid_in[0:UNITS, cells] = first.astype(bf16)
        mid_in[UNITS : 2 * UNITS, cells] = (slope * lin[:UNITS]).astype(bf16)
        mid_in[2 * UNITS :, cells] = (slope * lin[UNITS:]).astype(bf16)

    def layer_two(cells):
        lin = jnp.dot(wm[...], mid_in[:, cells], preferred_element_type=f32)
        second = jnp.tanh(lin[:UNITS] + bias[1])
        slope = 1.0 - second * second
        out_in[0:UNITS, cells] = (slope * lin[UNITS : 2 * UNITS]).astype(bf16)
        out_in[UNITS:, cells] = (slope * lin[2 * UNITS :]).astype(bf16)

    def layer_three(e, cells, keep):
        stress = jnp.dot(wo[...], out_in[:, cells], preferred_element_type=f32)
        stress = jnp.where(keep, stress, 0.0)
        v = st[e, :, cells]
        u = base[e, :, cells]
        g = []
        for j in range(3):
            u_j = base[e, j : j + 1, cells]
            v_j = jnp.where(upper_wide, st[e, j : j + 1, cells], st[e, 4 + j : 5 + j, cells])
            g.append(stress[8 * j : 8 * j + 8] - (u_j * v + v_j * u))
        return g

    for step in range(STEPS):
        lo, hi = 2 * step, EXT - 2 * step

        for start, planes, ref in (
            (0, HALO, base_low),
            (HALO, PLANES, base_own),
            (HALO + PLANES, HALO, base_high),
        ):

            @pl.loop(0, planes)
            def _(z):
                for k in range(parts):
                    rows = ref[z, step, k]
                    base[start + z, 0:4, k * LANES : (k + 1) * LANES] = rows
                    base[start + z, 4:8, k * LANES : (k + 1) * LANES] = rows

        def divergence(e, gx, gy):
            down_x, up_x = shift_x(gx, lane)
            for k in range(parts):
                down_y, up_y = shift_y(gy[k], column)
                part[e, :, k * LANES : (k + 1) * LANES] = (up_x[k] - down_x[k]) + (up_y - down_y)

        def update(e):
            new = st[e] + TIME_STEP * (part[e] + (gz[e + 1] - gz[e - 1]))
            if step == STEPS - 1:
                out[jnp.clip(e - HALO, 0, PLANES - 1)] = new
            else:
                st[e] = jnp.where(inside(e), new, 0.0)

        def body(i, ahead, one, two, three, after):
            gx, gy = [], []
            for n in range(PLANE // CHUNK):
                cells = slice(n * CHUNK, (n + 1) * CHUNK)
                if three:
                    g = layer_three(i - 4, cells, inside(i - 4))
                    gz[i - 4, :, cells] = g[2]
                    for half in range(CHUNK // LANES):
                        gx.append(g[0][:, half * LANES : (half + 1) * LANES])
                        gy.append(g[1][:, half * LANES : (half + 1) * LANES])
                if two:
                    layer_two(cells)
                if one:
                    layer_one(i - 2, cells)
            if three:
                divergence(i - 4, gx, gy)
            if ahead:
                patches(i)
            if after:
                update(i - 6)

        @pl.loop(lo, lo + 3)
        def _(i):
            body(i, True, False, False, False, False)

        body(lo + 3, True, True, False, False, False)
        body(lo + 4, True, True, True, False, False)

        @pl.loop(lo + 5, lo + 8)
        def _(i):
            body(i, True, True, True, True, False)

        @pl.loop(lo + 8, hi)
        def _(i):
            body(i, True, True, True, True, True)

        body(hi, False, True, True, True, True)
        body(hi + 1, False, False, True, True, True)
        body(hi + 2, False, False, False, True, True)
        body(hi + 3, False, False, False, False, True)


def weights_of(w_in, w_mid, w_out):
    bf16 = jnp.bfloat16
    eye = jnp.eye(2, dtype=bf16)
    split = jnp.pad(w_in.reshape(UNITS, 3, 9, 4), ((0, 0), (0, 0), (0, 1), (0, 0)))
    wp = eye[:, None, None, None, :, None] * split[None, :, :, :, None, :]
    wp = wp.reshape(2 * UNITS, 3 * PROWS)
    order = (0, 2, 3, 5, 6, 8, 1, 7, 4, 9, 9, 9)
    wb = jnp.concatenate([split[:, :, i : i + 1] for i in order], axis=2).reshape(UNITS, 3 * BROWS)
    wm = jnp.eye(3, dtype=bf16)[:, None, :, None] * w_mid[None, :, None, :]
    wm = wm.reshape(3 * UNITS, 3 * UNITS)
    out_pad = jnp.pad(w_out, ((0, 1), (0, 0)))
    comps = (0, 3, 4, 6, 3, 1, 5, 6, 4, 5, 2, 6)
    rows = jnp.concatenate([out_pad[i : i + 1] for i in comps], axis=0).reshape(3, 1, 4, 1, UNITS)
    wo = (rows * eye[None, :, None, :, None]).reshape(24, 2 * UNITS)
    return wp, wb, wm, wo


def take_plane(owner, come, mine):
    for s in range(STEPS):
        mine[s] = come[owner[s] & 15]


def take_copies(owner, place, c0, c1, c2, c3, send):
    for s in range(STEPS):
        turn = (place[2] - (owner[s] >> 4)) & 3
        chosen = jnp.where(turn == 1, c1[s], c0[s])
        chosen = jnp.where(turn == 2, c2[s], chosen)
        chosen = jnp.where(turn == 3, c3[s], chosen)
        for i in range(PLANES):
            send[i, s] = chosen


def spread_base(base_store, owner_steps, place, slabs):
    f32 = jnp.float32
    smem, vmem = (pl.BlockSpec(memory_space=m) for m in (pltpu.SMEM, pltpu.VMEM))
    tiles = jnp.transpose(base_store[0], (1, 0, 2)).reshape(PLANES, 4, 8, LANES)
    tiles = jnp.transpose(tiles, (0, 2, 1, 3))
    tiles = tiles.reshape(PLANES, 4, 8, LANES)
    come = lax.all_to_all(tiles, ("x", "y"), 0, 0, tiled=True)
    mine = pl.pallas_call(
        take_plane,
        out_shape=jax.ShapeDtypeStruct((STEPS, 4, 8, LANES), f32),
        in_specs=[smem, vmem],
        out_specs=vmem,
        compiler_params=pltpu.CompilerParams(vmem_limit_bytes=4 * 2**20),
    )(owner_steps, come)
    come = [mine] + [
        lax.ppermute(mine, "h", [(i, (i + k) % 4) for i in range(4)]) for k in (1, 2, 3)
    ]
    send = pl.pallas_call(
        take_copies,
        out_shape=jax.ShapeDtypeStruct((PLANES, STEPS, 4, 8, LANES), f32),
        in_specs=[smem, smem] + [vmem] * 4,
        out_specs=vmem,
        compiler_params=pltpu.CompilerParams(vmem_limit_bytes=4 * 2**20),
    )(owner_steps, place, *come)
    whole = lax.all_to_all(send, ("x", "y"), 0, 0, tiled=True)
    whole = whole.reshape(PLANES, STEPS, 8, 4, LANES)
    up = [(i, i + 1) for i in range(slabs - 1)]
    down = [(j, i) for i, j in up]
    low = lax.ppermute(whole[PLANES - HALO :], "gz", up)
    high = lax.ppermute(whole[:HALO], "gz", down)
    return low, whole, high


def local(base_store, perturbations, owner_steps, w_in, b_in, w_mid, b_mid, w_out):
    slabs = lax.axis_size("gz")
    slab = lax.axis_index("gz")
    state = jnp.transpose(perturbations.reshape(8, PLANES, PLANE), (1, 0, 2))
    up = [(i, i + 1) for i in range(slabs - 1)]
    down = [(j, i) for i, j in up]
    low = lax.ppermute(state[PLANES - HALO :], "gz", up)
    high = lax.ppermute(state[:HALO], "gz", down)
    place = jnp.stack([slab, jnp.int32(slabs), lax.axis_index("h")]).astype(jnp.int32)
    come = spread_base(base_store, owner_steps, place, slabs)
    vmem = pl.BlockSpec(memory_space=pltpu.VMEM)
    f32, bf16 = jnp.float32, jnp.bfloat16
    new = pl.pallas_call(
        kernel,
        out_shape=jax.ShapeDtypeStruct((PLANES, 8, PLANE), f32),
        in_specs=[pl.BlockSpec(memory_space=pltpu.SMEM)] + [vmem] * 12,
        out_specs=vmem,
        scratch_shapes=[
            pltpu.VMEM((EXT, 8, PLANE), f32),
            pltpu.VMEM((EXT, 8, PLANE), f32),
            pltpu.VMEM((EXT, PROWS, PLANE), bf16),
            pltpu.VMEM((EXT, BROWS, PLANE), bf16),
            pltpu.VMEM((EXT, 8, PLANE), f32),
            pltpu.VMEM((EXT, 8, PLANE), f32),
            pltpu.VMEM((2, UNITS, CHUNK), f32),
            pltpu.VMEM((3 * UNITS, PLANE), bf16),
            pltpu.VMEM((2 * UNITS, PLANE), bf16),
        ],
        compiler_params=pltpu.CompilerParams(vmem_limit_bytes=24 * 2**20),
    )(place, state, low, high, *come, *weights_of(w_in, w_mid, w_out), b_in[:, None], b_mid[:, None])
    return jnp.transpose(new, (1, 0, 2)).reshape(perturbations.shape)


def solution(mesh):
    spec = P(("h", "x", "y"), None, "gz", None)
    fine = Mesh(mesh.devices.reshape(4, 4, 4, mesh.devices.shape[1]), ("h", "x", "y", "gz"))
    in_specs = (spec, spec, P(), P(), P(), P(), P(), P())
    return jax.shard_map(local, mesh=fine, in_specs=in_specs, out_specs=spec, check_vma=False)
```

```python
import jax
import jax.numpy as jnp
from jax import lax
from jax.experimental import pallas as pl
from jax.experimental.pallas import tpu as pltpu
from jax.sharding import Mesh, PartitionSpec as P

NH = 32
STEPS = 3
TIME_STEP = 0.2
PLANES = 16
HALO = 6
EXT = PLANES + 2 * HALO
PLANE = 1024
UNITS = 64
LANES = 128
CHUNK = 256
PROWS = 80
BROWS = 48


def shift_y(v, column):
    up = jnp.where(column == NH - 1, pltpu.roll(v, NH - 1, 1), pltpu.roll(v, LANES - 1, 1))
    down = jnp.where(column == 0, pltpu.roll(v, LANES - NH + 1, 1), pltpu.roll(v, 1, 1))
    return down, up


def shift_x(parts, lane):
    n = len(parts)
    left = [pltpu.roll(v, LANES - NH, 1) for v in parts]
    right = [pltpu.roll(v, NH, 1) for v in parts]
    up = [jnp.where(lane < LANES - NH, left[k], left[(k + 1) % n]) for k in range(n)]
    down = [jnp.where(lane >= NH, right[k], right[(k - 1) % n]) for k in range(n)]
    return down, up


def kernel(place, own, low, high, base_low, base_own, base_high, wp, wb, wm, wo, b_in, b_mid, out,
           st, base, pp, bp, part, gz, bias, mid_in, out_in):
    f32, bf16 = jnp.float32, jnp.bfloat16
    lane = lax.broadcasted_iota(jnp.int32, (8, LANES), 1)
    column = lane % NH
    upper = lax.broadcasted_iota(jnp.int32, (8, LANES), 0) < 4
    upper_wide = lax.broadcasted_iota(jnp.int32, (8, CHUNK), 0) < 4
    parts = PLANE // LANES
    slab, slabs = place[0], place[1]

    st[0:HALO] = low[...]
    st[HALO : HALO + PLANES] = own[...]
    st[HALO + PLANES : EXT] = high[...]
    bias[0] = jnp.broadcast_to(b_in[...], (UNITS, CHUNK))
    bias[1] = jnp.broadcast_to(b_mid[...], (UNITS, CHUNK))
    pad = jnp.zeros((8, LANES), f32)

    def inside(e):
        level = slab * PLANES + e - HALO
        return jnp.logical_and(level >= 0, level < slabs * PLANES)

    def patches(e):
        mid = [st[e, :, k * LANES : (k + 1) * LANES] for k in range(parts)]
        moved = [shift_y(v, column) for v in mid]
        rows = []
        thirds = [[m[0] for m in moved], mid, [m[1] for m in moved]]
        moved_x = [shift_x(third, lane) for third in thirds]
        for xed in range(3):
            for yed in range(3):
                rows.append(thirds[yed] if xed == 1 else moved_x[yed][xed // 2])
        for t in range(5):
            for k in range(parts):
                second = rows[2 * t + 1][k] if 2 * t + 1 < 9 else pad
                pair = jnp.concatenate([rows[2 * t][k], second], axis=0)
                pp[e, 16 * t : 16 * t + 16, k * LANES : (k + 1) * LANES] = pair.astype(bf16)
        mid = [base[e, :, k * LANES : (k + 1) * LANES] for k in range(parts)]
        both = []
        for v in mid:
            down, up = shift_y(v, column)
            both.append(jnp.where(upper, down, up))
        both_down, both_up = shift_x(both, lane)
        mid_down, mid_up = shift_x(mid, lane)
        sides = [jnp.where(upper, a, b) for a, b in zip(mid_down, mid_up)]
        rows = [both_down, both, both_up, sides, mid, [pad] * parts]
        for t in range(3):
            for k in range(parts):
                pair = jnp.concatenate([rows[2 * t][k], rows[2 * t + 1][k]], axis=0)
                bp[e, 16 * t : 16 * t + 16, k * LANES : (k + 1) * LANES] = pair.astype(bf16)

    def layer_one(e, cells):
        patch = pp[pl.ds(e - 1, 3), :, cells].reshape(3 * PROWS, CHUNK)
        base_patch = bp[pl.ds(e - 1, 3), :, cells].reshape(3 * BROWS, CHUNK)
        first = jnp.tanh(jnp.dot(wb[...], base_patch, preferred_element_type=f32) + bias[0])
        slope = 1.0 - first * first
        lin = jnp.dot(wp[...], patch, preferred_element_type=f32)
        mid_in[0:UNITS, cells] = first.astype(bf16)
        mid_in[UNITS : 2 * UNITS, cells] = (slope * lin[:UNITS]).astype(bf16)
        mid_in[2 * UNITS :, cells] = (slope * lin[UNITS:]).astype(bf16)

    def layer_two(cells):
        def product(k):
            rows = slice(k * UNITS, (k + 1) * UNITS)
            return jnp.dot(wm[...], mid_in[rows, cells], preferred_element_type=f32)

        second = jnp.tanh(product(0) + bias[1])
        slope = 1.0 - second * second
        out_in[0:UNITS, cells] = (slope * product(1)).astype(bf16)
        out_in[UNITS:, cells] = (slope * product(2)).astype(bf16)

    def layer_three(e, cells, keep):
        stress = jnp.dot(wo[...], out_in[:, cells], preferred_element_type=f32)
        stress = jnp.where(keep, stress, 0.0)
        v = st[e, :, cells]
        u = base[e, :, cells]
        g = []
        for j in range(3):
            u_j = base[e, j : j + 1, cells]
            v_j = jnp.where(upper_wide, st[e, j : j + 1, cells], st[e, 4 + j : 5 + j, cells])
            g.append(stress[8 * j : 8 * j + 8] - (u_j * v + v_j * u))
        return g

    for step in range(STEPS):
        lo, hi = 2 * step, EXT - 2 * step

        for start, planes, ref in (
            (0, HALO, base_low),
            (HALO, PLANES, base_own),
            (HALO + PLANES, HALO, base_high),
        ):

            @pl.loop(0, planes)
            def _(z):
                for k in range(parts):
                    rows = ref[z, step, k]
                    base[start + z, 0:4, k * LANES : (k + 1) * LANES] = rows
                    base[start + z, 4:8, k * LANES : (k + 1) * LANES] = rows

        def divergence(e, gx, gy):
            down_x, up_x = shift_x(gx, lane)
            for k in range(parts):
                down_y, up_y = shift_y(gy[k], column)
                part[e, :, k * LANES : (k + 1) * LANES] = (up_x[k] - down_x[k]) + (up_y - down_y)

        def update(e):
            new = st[e] + TIME_STEP * (part[e] + (gz[e + 1] - gz[e - 1]))
            if step == STEPS - 1:
                out[jnp.clip(e - HALO, 0, PLANES - 1)] = new
            else:
                st[e] = jnp.where(inside(e), new, 0.0)

        def body(i, ahead, one, two, three, after):
            gx, gy = [], []
            cuts = [slice(n * CHUNK, (n + 1) * CHUNK) for n in range(PLANE // CHUNK)]
            if ahead:
                patches(i)
            if three:
                for cells in cuts:
                    g = layer_three(i - 4, cells, inside(i - 4))
                    gz[i - 4, :, cells] = g[2]
                    for half in range(CHUNK // LANES):
                        gx.append(g[0][:, half * LANES : (half + 1) * LANES])
                        gy.append(g[1][:, half * LANES : (half + 1) * LANES])
            if two:
                for cells in cuts:
                    layer_two(cells)
            if one:
                for cells in cuts:
                    layer_one(i - 2, cells)
            if three:
                divergence(i - 4, gx, gy)
            if after:
                update(i - 6)

        @pl.loop(lo, lo + 3)
        def _(i):
            body(i, True, False, False, False, False)

        body(lo + 3, True, True, False, False, False)
        body(lo + 4, True, True, True, False, False)

        @pl.loop(lo + 5, lo + 8)
        def _(i):
            body(i, True, True, True, True, False)

        @pl.loop(lo + 8, hi, unroll=2)
        def _(i):
            body(i, True, True, True, True, True)

        body(hi, False, True, True, True, True)
        body(hi + 1, False, False, True, True, True)
        body(hi + 2, False, False, False, True, True)
        body(hi + 3, False, False, False, False, True)


def weights_of(w_in, w_mid, w_out):
    bf16 = jnp.bfloat16
    eye = jnp.eye(2, dtype=bf16)
    split = jnp.pad(w_in.reshape(UNITS, 3, 9, 4), ((0, 0), (0, 0), (0, 1), (0, 0)))
    wp = eye[:, None, None, None, :, None] * split[None, :, :, :, None, :]
    wp = wp.reshape(2 * UNITS, 3 * PROWS)
    order = (0, 2, 3, 5, 6, 8, 1, 7, 4, 9, 9, 9)
    wb = jnp.concatenate([split[:, :, i : i + 1] for i in order], axis=2).reshape(UNITS, 3 * BROWS)
    out_pad = jnp.pad(w_out, ((0, 1), (0, 0)))
    comps = (0, 3, 4, 6, 3, 1, 5, 6, 4, 5, 2, 6)
    rows = jnp.concatenate([out_pad[i : i + 1] for i in comps], axis=0).reshape(3, 1, 4, 1, UNITS)
    wo = (rows * eye[None, :, None, :, None]).reshape(24, 2 * UNITS)
    return wp, wb, w_mid, wo


def regroup(planes, tiles):
    for field in range(4):
        for k in range(PLANE // LANES):
            rows = planes[field, :, k * LANES : (k + 1) * LANES]
            tiles[:, k // 2, 4 * (k % 2) + field, :] = rows


def take_plane(owner, come, mine):
    for s in range(STEPS):
        mine[s] = come[owner[s] & 15]


def take_copies(owner, place, c0, c1, c2, c3, send):
    for s in range(STEPS):
        turn = (place[2] - (owner[s] >> 4)) & 3
        chosen = jnp.where(turn == 1, c1[s], c0[s])
        chosen = jnp.where(turn == 2, c2[s], chosen)
        chosen = jnp.where(turn == 3, c3[s], chosen)
        for i in range(PLANES):
            send[i, s] = chosen


def spread_base(base_store, owner_steps, place, slabs):
    f32 = jnp.float32
    smem, vmem = (pl.BlockSpec(memory_space=m) for m in (pltpu.SMEM, pltpu.VMEM))
    tiles = pl.pallas_call(
        regroup,
        out_shape=jax.ShapeDtypeStruct((PLANES, 4, 8, LANES), f32),
        in_specs=[vmem],
        out_specs=vmem,
        compiler_params=pltpu.CompilerParams(vmem_limit_bytes=4 * 2**20),
    )(base_store[0])
    come = lax.all_to_all(tiles, ("x", "y"), 0, 0, tiled=True)
    mine = pl.pallas_call(
        take_plane,
        out_shape=jax.ShapeDtypeStruct((STEPS, 4, 8, LANES), f32),
        in_specs=[smem, vmem],
        out_specs=vmem,
        compiler_params=pltpu.CompilerParams(vmem_limit_bytes=4 * 2**20),
    )(owner_steps, come)
    come = [mine] + [
        lax.ppermute(mine, "h", [(i, (i + k) % 4) for i in range(4)]) for k in (1, 2, 3)
    ]
    send = pl.pallas_call(
        take_copies,
        out_shape=jax.ShapeDtypeStruct((PLANES, STEPS, 4, 8, LANES), f32),
        in_specs=[smem, smem] + [vmem] * 4,
        out_specs=vmem,
        compiler_params=pltpu.CompilerParams(vmem_limit_bytes=4 * 2**20),
    )(owner_steps, place, *come)
    whole = lax.all_to_all(send, ("x", "y"), 0, 0, tiled=True)
    whole = whole.reshape(PLANES, STEPS, 8, 4, LANES)
    up = [(i, i + 1) for i in range(slabs - 1)]
    down = [(j, i) for i, j in up]
    low = lax.ppermute(whole[PLANES - HALO :], "gz", up)
    high = lax.ppermute(whole[:HALO], "gz", down)
    return low, whole, high


def local(base_store, perturbations, owner_steps, w_in, b_in, w_mid, b_mid, w_out):
    slabs = lax.axis_size("gz")
    slab = lax.axis_index("gz")
    state = jnp.transpose(perturbations.reshape(8, PLANES, PLANE), (1, 0, 2))
    up = [(i, i + 1) for i in range(slabs - 1)]
    down = [(j, i) for i, j in up]
    low = lax.ppermute(state[PLANES - HALO :], "gz", up)
    high = lax.ppermute(state[:HALO], "gz", down)
    place = jnp.stack([slab, jnp.int32(slabs), lax.axis_index("h")]).astype(jnp.int32)
    come = spread_base(base_store, owner_steps, place, slabs)
    vmem = pl.BlockSpec(memory_space=pltpu.VMEM)
    f32, bf16 = jnp.float32, jnp.bfloat16
    new = pl.pallas_call(
        kernel,
        out_shape=jax.ShapeDtypeStruct((PLANES, 8, PLANE), f32),
        in_specs=[pl.BlockSpec(memory_space=pltpu.SMEM)] + [vmem] * 12,
        out_specs=vmem,
        scratch_shapes=[
            pltpu.VMEM((EXT, 8, PLANE), f32),
            pltpu.VMEM((EXT, 8, PLANE), f32),
            pltpu.VMEM((EXT, PROWS, PLANE), bf16),
            pltpu.VMEM((EXT, BROWS, PLANE), bf16),
            pltpu.VMEM((EXT, 8, PLANE), f32),
            pltpu.VMEM((EXT, 8, PLANE), f32),
            pltpu.VMEM((2, UNITS, CHUNK), f32),
            pltpu.VMEM((3 * UNITS, PLANE), bf16),
            pltpu.VMEM((2 * UNITS, PLANE), bf16),
        ],
        compiler_params=pltpu.CompilerParams(vmem_limit_bytes=24 * 2**20),
    )(place, state, low, high, *come, *weights_of(w_in, w_mid, w_out), b_in[:, None], b_mid[:, None])
    return jnp.transpose(new, (1, 0, 2)).reshape(perturbations.shape)


def solution(mesh):
    spec = P(("h", "x", "y"), None, "gz", None)
    fine = Mesh(mesh.devices.reshape(4, 4, 4, mesh.devices.shape[1]), ("h", "x", "y", "gz"))
    in_specs = (spec, spec, P(), P(), P(), P(), P(), P())
    return jax.shard_map(local, mesh=fine, in_specs=in_specs, out_specs=spec, check_vma=False)
```

```python
import jax
import jax.numpy as jnp
from jax import lax
from jax.experimental import pallas as pl
from jax.experimental.pallas import tpu as pltpu
from jax.sharding import Mesh, PartitionSpec as P

NH = 32
STEPS = 3
TIME_STEP = 0.2
PLANES = 16
HALO = 6
EXT = PLANES + 2 * HALO
PLANE = 1024
UNITS = 64
LANES = 128
CHUNK = 256
PROWS = 80
BROWS = 48


def shift_y(v, column):
    up = jnp.where(column == NH - 1, pltpu.roll(v, NH - 1, 1), pltpu.roll(v, LANES - 1, 1))
    down = jnp.where(column == 0, pltpu.roll(v, LANES - NH + 1, 1), pltpu.roll(v, 1, 1))
    return down, up


def shift_x(parts, lane):
    n = len(parts)
    left = [pltpu.roll(v, LANES - NH, 1) for v in parts]
    right = [pltpu.roll(v, NH, 1) for v in parts]
    up = [jnp.where(lane < LANES - NH, left[k], left[(k + 1) % n]) for k in range(n)]
    down = [jnp.where(lane >= NH, right[k], right[(k - 1) % n]) for k in range(n)]
    return down, up


def kernel(place, own, low, high, base_low, base_own, base_high, wp, wb, wm, wo, b_in, b_mid, out,
           st, base, pp, bp, part, gz, bias, mid_in, out_in):
    f32, bf16 = jnp.float32, jnp.bfloat16
    lane = lax.broadcasted_iota(jnp.int32, (8, LANES), 1)
    column = lane % NH
    upper = lax.broadcasted_iota(jnp.int32, (8, LANES), 0) < 4
    upper_wide = lax.broadcasted_iota(jnp.int32, (8, CHUNK), 0) < 4
    parts = PLANE // LANES
    slab, slabs = place[0], place[1]

    st[0:HALO] = low[...]
    st[HALO : HALO + PLANES] = own[...]
    st[HALO + PLANES : EXT] = high[...]
    bias[0] = jnp.broadcast_to(b_in[...], (UNITS, CHUNK))
    bias[1] = jnp.broadcast_to(b_mid[...], (UNITS, CHUNK))
    pad = jnp.zeros((8, LANES), f32)

    def inside(e):
        level = slab * PLANES + e - HALO
        return jnp.logical_and(level >= 0, level < slabs * PLANES)

    def patches(e):
        mid = [st[e, :, k * LANES : (k + 1) * LANES] for k in range(parts)]
        moved = [shift_y(v, column) for v in mid]
        rows = []
        thirds = [[m[0] for m in moved], mid, [m[1] for m in moved]]
        moved_x = [shift_x(third, lane) for third in thirds]
        for xed in range(3):
            for yed in range(3):
                rows.append(thirds[yed] if xed == 1 else moved_x[yed][xed // 2])
        for t in range(5):
            for k in range(parts):
                second = rows[2 * t + 1][k] if 2 * t + 1 < 9 else pad
                pair = jnp.concatenate([rows[2 * t][k], second], axis=0)
                pp[e, 16 * t : 16 * t + 16, k * LANES : (k + 1) * LANES] = pair.astype(bf16)
        mid = [base[e, :, k * LANES : (k + 1) * LANES] for k in range(parts)]
        both = []
        for v in mid:
            down, up = shift_y(v, column)
            both.append(jnp.where(upper, down, up))
        both_down, both_up = shift_x(both, lane)
        mid_down, mid_up = shift_x(mid, lane)
        sides = [jnp.where(upper, a, b) for a, b in zip(mid_down, mid_up)]
        rows = [both_down, both, both_up, sides, mid, [pad] * parts]
        for t in range(3):
            for k in range(parts):
                pair = jnp.concatenate([rows[2 * t][k], rows[2 * t + 1][k]], axis=0)
                bp[e, 16 * t : 16 * t + 16, k * LANES : (k + 1) * LANES] = pair.astype(bf16)

    def layer_one(e, cells):
        patch = pp[pl.ds(e - 1, 3), :, cells].reshape(3 * PROWS, CHUNK)
        base_patch = bp[pl.ds(e - 1, 3), :, cells].reshape(3 * BROWS, CHUNK)
        first = jnp.tanh(jnp.dot(wb[...], base_patch, preferred_element_type=f32) + bias[0])
        slope = 1.0 - first * first
        lin = jnp.dot(wp[...], patch, preferred_element_type=f32)
        mid_in[0:UNITS, cells] = first.astype(bf16)
        mid_in[UNITS : 2 * UNITS, cells] = (slope * lin[:UNITS]).astype(bf16)
        mid_in[2 * UNITS :, cells] = (slope * lin[UNITS:]).astype(bf16)

    def layer_two(cells):
        def product(k):
            rows = slice(k * UNITS, (k + 1) * UNITS)
            return jnp.dot(wm[...], mid_in[rows, cells], preferred_element_type=f32)

        second = jnp.tanh(product(0) + bias[1])
        slope = 1.0 - second * second
        out_in[0:UNITS, cells] = (slope * product(1)).astype(bf16)
        out_in[UNITS:, cells] = (slope * product(2)).astype(bf16)

    def layer_three(e, cells, keep):
        stress = jnp.dot(wo[...], out_in[:, cells], preferred_element_type=f32)
        stress = jnp.where(keep, stress, 0.0)
        v = st[e, :, cells]
        u = base[e, :, cells]
        g = []
        for j in range(3):
            u_j = base[e, j : j + 1, cells]
            v_j = jnp.where(upper_wide, st[e, j : j + 1, cells], st[e, 4 + j : 5 + j, cells])
            g.append(stress[8 * j : 8 * j + 8] - (u_j * v + v_j * u))
        return g

    for step in range(STEPS):
        lo, hi = 2 * step, EXT - 2 * step

        for start, planes, ref in (
            (0, HALO, base_low),
            (HALO, PLANES, base_own),
            (HALO + PLANES, HALO, base_high),
        ):

            @pl.loop(0, planes, unroll=2)
            def _(z):
                for k in range(parts):
                    rows = ref[z, step, k]
                    base[start + z, 0:4, k * LANES : (k + 1) * LANES] = rows
                    base[start + z, 4:8, k * LANES : (k + 1) * LANES] = rows

        def divergence(e, gx, gy):
            down_x, up_x = shift_x(gx, lane)
            for k in range(parts):
                down_y, up_y = shift_y(gy[k], column)
                part[e, :, k * LANES : (k + 1) * LANES] = (up_x[k] - down_x[k]) + (up_y - down_y)

        def update(e):
            new = st[e] + TIME_STEP * (part[e] + (gz[e + 1] - gz[e - 1]))
            if step == STEPS - 1:
                out[jnp.clip(e - HALO, 0, PLANES - 1)] = new
            else:
                st[e] = jnp.where(inside(e), new, 0.0)

        def body(i, ahead, one, two, three, after):
            gx, gy = [], []
            cuts = [slice(n * CHUNK, (n + 1) * CHUNK) for n in range(PLANE // CHUNK)]
            if ahead:
                patches(i)
            if three:
                for cells in cuts:
                    g = layer_three(i - 4, cells, inside(i - 4))
                    gz[i - 4, :, cells] = g[2]
                    for half in range(CHUNK // LANES):
                        gx.append(g[0][:, half * LANES : (half + 1) * LANES])
                        gy.append(g[1][:, half * LANES : (half + 1) * LANES])
            if two:
                for cells in cuts:
                    layer_two(cells)
            if one:
                for cells in cuts:
                    layer_one(i - 2, cells)
            if three:
                divergence(i - 4, gx, gy)
            if after:
                update(i - 6)

        @pl.loop(lo, lo + 3, unroll=3)
        def _(i):
            body(i, True, False, False, False, False)

        body(lo + 3, True, True, False, False, False)
        body(lo + 4, True, True, True, False, False)

        @pl.loop(lo + 5, lo + 8, unroll=3)
        def _(i):
            body(i, True, True, True, True, False)

        @pl.loop(lo + 8, hi, unroll=4)
        def _(i):
            body(i, True, True, True, True, True)

        body(hi, False, True, True, True, True)
        body(hi + 1, False, False, True, True, True)
        body(hi + 2, False, False, False, True, True)
        body(hi + 3, False, False, False, False, True)


def weights_of(w_in, w_mid, w_out):
    bf16 = jnp.bfloat16
    eye = jnp.eye(2, dtype=bf16)
    split = jnp.pad(w_in.reshape(UNITS, 3, 9, 4), ((0, 0), (0, 0), (0, 1), (0, 0)))
    wp = eye[:, None, None, None, :, None] * split[None, :, :, :, None, :]
    wp = wp.reshape(2 * UNITS, 3 * PROWS)
    order = (0, 2, 3, 5, 6, 8, 1, 7, 4, 9, 9, 9)
    wb = jnp.concatenate([split[:, :, i : i + 1] for i in order], axis=2).reshape(UNITS, 3 * BROWS)
    out_pad = jnp.pad(w_out, ((0, 1), (0, 0)))
    comps = (0, 3, 4, 6, 3, 1, 5, 6, 4, 5, 2, 6)
    rows = jnp.concatenate([out_pad[i : i + 1] for i in comps], axis=0).reshape(3, 1, 4, 1, UNITS)
    wo = (rows * eye[None, :, None, :, None]).reshape(24, 2 * UNITS)
    return wp, wb, w_mid, wo


def regroup(planes, tiles):
    for field in range(4):
        for k in range(PLANE // LANES):
            rows = planes[field, :, k * LANES : (k + 1) * LANES]
            tiles[:, k // 2, 4 * (k % 2) + field, :] = rows


def take_plane(owner, come, mine):
    for s in range(STEPS):
        mine[s] = come[owner[s] & 15]


def take_copies(owner, place, c0, c1, c2, c3, send):
    for s in range(STEPS):
        turn = (place[2] - (owner[s] >> 4)) & 3
        chosen = jnp.where(turn == 1, c1[s], c0[s])
        chosen = jnp.where(turn == 2, c2[s], chosen)
        chosen = jnp.where(turn == 3, c3[s], chosen)
        for i in range(PLANES):
            send[i, s] = chosen


def spread_base(base_store, owner_steps, place, slabs):
    f32 = jnp.float32
    smem, vmem = (pl.BlockSpec(memory_space=m) for m in (pltpu.SMEM, pltpu.VMEM))
    tiles = pl.pallas_call(
        regroup,
        out_shape=jax.ShapeDtypeStruct((PLANES, 4, 8, LANES), f32),
        in_specs=[vmem],
        out_specs=vmem,
        compiler_params=pltpu.CompilerParams(vmem_limit_bytes=4 * 2**20),
    )(base_store[0])
    come = lax.all_to_all(tiles, ("x", "y"), 0, 0, tiled=True)
    mine = pl.pallas_call(
        take_plane,
        out_shape=jax.ShapeDtypeStruct((STEPS, 4, 8, LANES), f32),
        in_specs=[smem, vmem],
        out_specs=vmem,
        compiler_params=pltpu.CompilerParams(vmem_limit_bytes=4 * 2**20),
    )(owner_steps, come)
    come = [mine] + [
        lax.ppermute(mine, "h", [(i, (i + k) % 4) for i in range(4)]) for k in (1, 2, 3)
    ]
    send = pl.pallas_call(
        take_copies,
        out_shape=jax.ShapeDtypeStruct((PLANES, STEPS, 4, 8, LANES), f32),
        in_specs=[smem, smem] + [vmem] * 4,
        out_specs=vmem,
        compiler_params=pltpu.CompilerParams(vmem_limit_bytes=4 * 2**20),
    )(owner_steps, place, *come)
    whole = lax.all_to_all(send, ("x", "y"), 0, 0, tiled=True)
    whole = whole.reshape(PLANES, STEPS, 8, 4, LANES)
    up = [(i, i + 1) for i in range(slabs - 1)]
    down = [(j, i) for i, j in up]
    low = lax.ppermute(whole[PLANES - HALO :], "gz", up)
    high = lax.ppermute(whole[:HALO], "gz", down)
    return low, whole, high


def local(base_store, perturbations, owner_steps, w_in, b_in, w_mid, b_mid, w_out):
    slabs = lax.axis_size("gz")
    slab = lax.axis_index("gz")
    state = jnp.transpose(perturbations.reshape(8, PLANES, PLANE), (1, 0, 2))
    up = [(i, i + 1) for i in range(slabs - 1)]
    down = [(j, i) for i, j in up]
    low = lax.ppermute(state[PLANES - HALO :], "gz", up)
    high = lax.ppermute(state[:HALO], "gz", down)
    place = jnp.stack([slab, jnp.int32(slabs), lax.axis_index("h")]).astype(jnp.int32)
    come = spread_base(base_store, owner_steps, place, slabs)
    vmem = pl.BlockSpec(memory_space=pltpu.VMEM)
    f32, bf16 = jnp.float32, jnp.bfloat16
    new = pl.pallas_call(
        kernel,
        out_shape=jax.ShapeDtypeStruct((PLANES, 8, PLANE), f32),
        in_specs=[pl.BlockSpec(memory_space=pltpu.SMEM)] + [vmem] * 12,
        out_specs=vmem,
        scratch_shapes=[
            pltpu.VMEM((EXT, 8, PLANE), f32),
            pltpu.VMEM((EXT, 8, PLANE), f32),
            pltpu.VMEM((EXT, PROWS, PLANE), bf16),
            pltpu.VMEM((EXT, BROWS, PLANE), bf16),
            pltpu.VMEM((EXT, 8, PLANE), f32),
            pltpu.VMEM((EXT, 8, PLANE), f32),
            pltpu.VMEM((2, UNITS, CHUNK), f32),
            pltpu.VMEM((3 * UNITS, PLANE), bf16),
            pltpu.VMEM((2 * UNITS, PLANE), bf16),
        ],
        compiler_params=pltpu.CompilerParams(vmem_limit_bytes=24 * 2**20),
    )(place, state, low, high, *come, *weights_of(w_in, w_mid, w_out), b_in[:, None], b_mid[:, None])
    return jnp.transpose(new, (1, 0, 2)).reshape(perturbations.shape)


def solution(mesh):
    spec = P(("h", "x", "y"), None, "gz", None)
    fine = Mesh(mesh.devices.reshape(4, 4, 4, mesh.devices.shape[1]), ("h", "x", "y", "gz"))
    in_specs = (spec, spec, P(), P(), P(), P(), P(), P())
    return jax.shard_map(local, mesh=fine, in_specs=in_specs, out_specs=spec, check_vma=False)
```

```python
import jax
import jax.numpy as jnp
from jax import lax
from jax.experimental import pallas as pl
from jax.experimental.pallas import tpu as pltpu
from jax.sharding import Mesh, PartitionSpec as P

NH = 32
STEPS = 3
TIME_STEP = 0.2
PLANES = 16
HALO = 6
EXT = PLANES + 2 * HALO
PLANE = 1024
UNITS = 64
LANES = 128
CHUNK = 256
PROWS = 80
BROWS = 48


def shift_y(v, column):
    up = jnp.where(column == NH - 1, pltpu.roll(v, NH - 1, 1), pltpu.roll(v, LANES - 1, 1))
    down = jnp.where(column == 0, pltpu.roll(v, LANES - NH + 1, 1), pltpu.roll(v, 1, 1))
    return down, up


def shift_x(parts, lane):
    n = len(parts)
    left = [pltpu.roll(v, LANES - NH, 1) for v in parts]
    right = [pltpu.roll(v, NH, 1) for v in parts]
    up = [jnp.where(lane < LANES - NH, left[k], left[(k + 1) % n]) for k in range(n)]
    down = [jnp.where(lane >= NH, right[k], right[(k - 1) % n]) for k in range(n)]
    return down, up


def kernel(place, own, low, high, base_low, base_own, base_high, wp, wb, wm, wo, b_in, b_mid, out,
           st, base, pp, bp, part, gz, bias, mid_in, out_in):
    f32, bf16 = jnp.float32, jnp.bfloat16
    lane = lax.broadcasted_iota(jnp.int32, (8, LANES), 1)
    column = lane % NH
    upper = lax.broadcasted_iota(jnp.int32, (8, LANES), 0) < 4
    upper_wide = lax.broadcasted_iota(jnp.int32, (8, CHUNK), 0) < 4
    parts = PLANE // LANES
    slab, slabs = place[0], place[1]

    st[0:HALO] = low[...]
    st[HALO : HALO + PLANES] = own[...]
    st[HALO + PLANES : EXT] = high[...]
    bias[0] = jnp.broadcast_to(b_in[...], (UNITS, CHUNK))
    bias[1] = jnp.broadcast_to(b_mid[...], (UNITS, CHUNK))
    pad = jnp.zeros((8, LANES), f32)

    def inside(e):
        level = slab * PLANES + e - HALO
        return jnp.logical_and(level >= 0, level < slabs * PLANES)

    def patches(e):
        mid = [st[e, :, k * LANES : (k + 1) * LANES] for k in range(parts)]
        moved = [shift_y(v, column) for v in mid]
        rows = []
        thirds = [[m[0] for m in moved], mid, [m[1] for m in moved]]
        moved_x = [shift_x(third, lane) for third in thirds]
        for xed in range(3):
            for yed in range(3):
                rows.append(thirds[yed] if xed == 1 else moved_x[yed][xed // 2])
        for t in range(5):
            for k in range(parts):
                second = rows[2 * t + 1][k] if 2 * t + 1 < 9 else pad
                pair = jnp.concatenate([rows[2 * t][k], second], axis=0)
                pp[e, 16 * t : 16 * t + 16, k * LANES : (k + 1) * LANES] = pair.astype(bf16)
        mid = [base[e, :, k * LANES : (k + 1) * LANES] for k in range(parts)]
        both = []
        for v in mid:
            down, up = shift_y(v, column)
            both.append(jnp.where(upper, down, up))
        both_down, both_up = shift_x(both, lane)
        mid_down, mid_up = shift_x(mid, lane)
        sides = [jnp.where(upper, a, b) for a, b in zip(mid_down, mid_up)]
        rows = [both_down, both, both_up, sides, mid, [pad] * parts]
        for t in range(3):
            for k in range(parts):
                pair = jnp.concatenate([rows[2 * t][k], rows[2 * t + 1][k]], axis=0)
                bp[e, 16 * t : 16 * t + 16, k * LANES : (k + 1) * LANES] = pair.astype(bf16)

    def layer_one(e, cells):
        patch = pp[pl.ds(e - 1, 3), :, cells].reshape(3 * PROWS, CHUNK)
        base_patch = bp[pl.ds(e - 1, 3), :, cells].reshape(3 * BROWS, CHUNK)
        first = jnp.tanh(jnp.dot(wb[...], base_patch, preferred_element_type=f32) + bias[0])
        slope = 1.0 - first * first
        lin = jnp.dot(wp[...], patch, preferred_element_type=f32)
        mid_in[0:UNITS, cells] = first.astype(bf16)
        mid_in[UNITS : 2 * UNITS, cells] = (slope * lin[:UNITS]).astype(bf16)
        mid_in[2 * UNITS :, cells] = (slope * lin[UNITS:]).astype(bf16)

    def layer_two(cells):
        def product(k):
            rows = slice(k * UNITS, (k + 1) * UNITS)
            return jnp.dot(wm[...], mid_in[rows, cells], preferred_element_type=f32)

        second = jnp.tanh(product(0) + bias[1])
        slope = 1.0 - second * second
        out_in[0:UNITS, cells] = (slope * product(1)).astype(bf16)
        out_in[UNITS:, cells] = (slope * product(2)).astype(bf16)

    def layer_three(e, cells, keep):
        stress = jnp.dot(wo[...], out_in[:, cells], preferred_element_type=f32)
        stress = jnp.where(keep, stress, 0.0)
        v = st[e, :, cells]
        u = base[e, :, cells]
        g = []
        for j in range(3):
            u_j = base[e, j : j + 1, cells]
            v_j = jnp.where(upper_wide, st[e, j : j + 1, cells], st[e, 4 + j : 5 + j, cells])
            g.append(stress[8 * j : 8 * j + 8] - (u_j * v + v_j * u))
        return g

    for step in range(STEPS):
        lo, hi = 2 * step, EXT - 2 * step

        for start, planes, ref in (
            (0, HALO, base_low),
            (HALO, PLANES, base_own),
            (HALO + PLANES, HALO, base_high),
        ):

            @pl.loop(0, planes, unroll=2)
            def _(z):
                for k in range(parts):
                    rows = ref[z, step, k]
                    base[start + z, 0:4, k * LANES : (k + 1) * LANES] = rows
                    base[start + z, 4:8, k * LANES : (k + 1) * LANES] = rows

        def divergence(e, gx, gy):
            down_x, up_x = shift_x(gx, lane)
            for k in range(parts):
                down_y, up_y = shift_y(gy[k], column)
                part[e, :, k * LANES : (k + 1) * LANES] = (up_x[k] - down_x[k]) + (up_y - down_y)

        def update(e):
            new = st[e] + TIME_STEP * (part[e] + (gz[e + 1] - gz[e - 1]))
            if step == STEPS - 1:
                out[jnp.clip(e - HALO, 0, PLANES - 1)] = new
            else:
                st[e] = jnp.where(inside(e), new, 0.0)

        def body(i, ahead, one, two, three, after):
            gx, gy = [], []
            cuts = [slice(n * CHUNK, (n + 1) * CHUNK) for n in range(PLANE // CHUNK)]
            if ahead:
                patches(i)
            if three:
                for cells in cuts:
                    g = layer_three(i - 4, cells, inside(i - 4))
                    gz[i - 4, :, cells] = g[2]
                    for half in range(CHUNK // LANES):
                        gx.append(g[0][:, half * LANES : (half + 1) * LANES])
                        gy.append(g[1][:, half * LANES : (half + 1) * LANES])
            if two:
                for cells in cuts:
                    layer_two(cells)
            if one:
                for cells in cuts:
                    layer_one(i - 2, cells)
            if three:
                divergence(i - 4, gx, gy)
            if after:
                update(i - 6)

        @pl.loop(lo, lo + 3, unroll=3)
        def _(i):
            body(i, True, False, False, False, False)

        body(lo + 3, True, True, False, False, False)
        body(lo + 4, True, True, True, False, False)

        @pl.loop(lo + 5, lo + 8, unroll=3)
        def _(i):
            body(i, True, True, True, True, False)

        @pl.loop(lo + 8, hi, unroll=(5, 8, 6)[step])
        def _(i):
            body(i, True, True, True, True, True)

        body(hi, False, True, True, True, True)
        body(hi + 1, False, False, True, True, True)
        body(hi + 2, False, False, False, True, True)
        body(hi + 3, False, False, False, False, True)


def weights_of(w_in, w_mid, w_out):
    bf16 = jnp.bfloat16
    eye = jnp.eye(2, dtype=bf16)
    split = jnp.pad(w_in.reshape(UNITS, 3, 9, 4), ((0, 0), (0, 0), (0, 1), (0, 0)))
    wp = eye[:, None, None, None, :, None] * split[None, :, :, :, None, :]
    wp = wp.reshape(2 * UNITS, 3 * PROWS)
    order = (0, 2, 3, 5, 6, 8, 1, 7, 4, 9, 9, 9)
    wb = jnp.concatenate([split[:, :, i : i + 1] for i in order], axis=2).reshape(UNITS, 3 * BROWS)
    out_pad = jnp.pad(w_out, ((0, 1), (0, 0)))
    comps = (0, 3, 4, 6, 3, 1, 5, 6, 4, 5, 2, 6)
    rows = jnp.concatenate([out_pad[i : i + 1] for i in comps], axis=0).reshape(3, 1, 4, 1, UNITS)
    wo = (rows * eye[None, :, None, :, None]).reshape(24, 2 * UNITS)
    return wp, wb, w_mid, wo


def regroup(planes, tiles):
    for field in range(4):
        for k in range(PLANE // LANES):
            rows = planes[field, :, k * LANES : (k + 1) * LANES]
            tiles[:, k // 2, 4 * (k % 2) + field, :] = rows


def take_plane(owner, come, mine):
    for s in range(STEPS):
        mine[s] = come[owner[s] & 15]


def take_copies(owner, place, c0, c1, c2, c3, send):
    for s in range(STEPS):
        turn = (place[2] - (owner[s] >> 4)) & 3
        chosen = jnp.where(turn == 1, c1[s], c0[s])
        chosen = jnp.where(turn == 2, c2[s], chosen)
        chosen = jnp.where(turn == 3, c3[s], chosen)
        for i in range(PLANES):
            send[i, s] = chosen


def spread_base(base_store, owner_steps, place, slabs):
    f32 = jnp.float32
    smem, vmem = (pl.BlockSpec(memory_space=m) for m in (pltpu.SMEM, pltpu.VMEM))
    tiles = pl.pallas_call(
        regroup,
        out_shape=jax.ShapeDtypeStruct((PLANES, 4, 8, LANES), f32),
        in_specs=[vmem],
        out_specs=vmem,
        compiler_params=pltpu.CompilerParams(vmem_limit_bytes=4 * 2**20),
    )(base_store[0])
    come = lax.all_to_all(tiles, ("x", "y"), 0, 0, tiled=True)
    mine = pl.pallas_call(
        take_plane,
        out_shape=jax.ShapeDtypeStruct((STEPS, 4, 8, LANES), f32),
        in_specs=[smem, vmem],
        out_specs=vmem,
        compiler_params=pltpu.CompilerParams(vmem_limit_bytes=4 * 2**20),
    )(owner_steps, come)
    come = [mine] + [
        lax.ppermute(mine, "h", [(i, (i + k) % 4) for i in range(4)]) for k in (1, 2, 3)
    ]
    send = pl.pallas_call(
        take_copies,
        out_shape=jax.ShapeDtypeStruct((PLANES, STEPS, 4, 8, LANES), f32),
        in_specs=[smem, smem] + [vmem] * 4,
        out_specs=vmem,
        compiler_params=pltpu.CompilerParams(vmem_limit_bytes=4 * 2**20),
    )(owner_steps, place, *come)
    whole = lax.all_to_all(send, ("x", "y"), 0, 0, tiled=True)
    whole = whole.reshape(PLANES, STEPS, 8, 4, LANES)
    up = [(i, i + 1) for i in range(slabs - 1)]
    down = [(j, i) for i, j in up]
    low = lax.ppermute(whole[PLANES - HALO :], "gz", up)
    high = lax.ppermute(whole[:HALO], "gz", down)
    return low, whole, high


def local(base_store, perturbations, owner_steps, w_in, b_in, w_mid, b_mid, w_out):
    slabs = lax.axis_size("gz")
    slab = lax.axis_index("gz")
    state = jnp.transpose(perturbations.reshape(8, PLANES, PLANE), (1, 0, 2))
    up = [(i, i + 1) for i in range(slabs - 1)]
    down = [(j, i) for i, j in up]
    low = lax.ppermute(state[PLANES - HALO :], "gz", up)
    high = lax.ppermute(state[:HALO], "gz", down)
    place = jnp.stack([slab, jnp.int32(slabs), lax.axis_index("h")]).astype(jnp.int32)
    come = spread_base(base_store, owner_steps, place, slabs)
    vmem = pl.BlockSpec(memory_space=pltpu.VMEM)
    f32, bf16 = jnp.float32, jnp.bfloat16
    new = pl.pallas_call(
        kernel,
        out_shape=jax.ShapeDtypeStruct((PLANES, 8, PLANE), f32),
        in_specs=[pl.BlockSpec(memory_space=pltpu.SMEM)] + [vmem] * 12,
        out_specs=vmem,
        scratch_shapes=[
            pltpu.VMEM((EXT, 8, PLANE), f32),
            pltpu.VMEM((EXT, 8, PLANE), f32),
            pltpu.VMEM((EXT, PROWS, PLANE), bf16),
            pltpu.VMEM((EXT, BROWS, PLANE), bf16),
            pltpu.VMEM((EXT, 8, PLANE), f32),
            pltpu.VMEM((EXT, 8, PLANE), f32),
            pltpu.VMEM((2, UNITS, CHUNK), f32),
            pltpu.VMEM((3 * UNITS, PLANE), bf16),
            pltpu.VMEM((2 * UNITS, PLANE), bf16),
        ],
        compiler_params=pltpu.CompilerParams(vmem_limit_bytes=24 * 2**20),
    )(place, state, low, high, *come, *weights_of(w_in, w_mid, w_out), b_in[:, None], b_mid[:, None])
    return jnp.transpose(new, (1, 0, 2)).reshape(perturbations.shape)


def solution(mesh):
    spec = P(("h", "x", "y"), None, "gz", None)
    fine = Mesh(mesh.devices.reshape(4, 4, 4, mesh.devices.shape[1]), ("h", "x", "y", "gz"))
    in_specs = (spec, spec, P(), P(), P(), P(), P(), P())
    return jax.shard_map(local, mesh=fine, in_specs=in_specs, out_specs=spec, check_vma=False)
```
